1024 devices in a mesh: grid: 256 (over z, y, x_hi), layer: 4 (over x_lo, core).
Axes of the slice: x: 4 (x_hi: 2, x_lo: 2; x = x_hi * 2 + x_lo), y: 8, z: 16, core: 2. Of those that a mesh axis runs over, the one named last changes fastest.
Arguments:
- x_panel: bfloat16 [65536, 256], P(('grid', 'layer')), may hold values from -6 to 6
- b_panel: bfloat16 [65536, 256], P(('grid', 'layer')), may hold values from -6 to 6
- a_blocks: bfloat16 [1024, 4, 64, 64, 64], P('grid', 'layer'), may hold values from -0.046875 to 0.046875
- a_inner: int32 [1024, 4, 64], P('grid', 'layer'), may hold values from 0 to 255, as said below
- a_count: int32 [1024, 4], P('grid', 'layer'), may hold values from 16 to 64, as said below
Outputs:
- new_panel: bfloat16 [65536, 256], P(('grid', 'layer'))
The draws below stay inside these ranges and needn't reach their ends.
Inputs may be any that keep to these rules, and one draw needn't show every extreme that they name: `a_inner`: within each row cluster and layer the entries are distinct and ascending. `a_count`: some row cluster and layer has all 64 slots live in every draw.
All inputs are finite; a program needn't handle non-finite values.
Results may differ from the reference program's by a relative error of at most 0.001.
Values may be sent and summed in bfloat16 or wider, within the bound.
No kernel may reach another device: no remote copies, remote signals or barrier semaphores. Data moves between devices by JAX's collectives and lax.ppermute only.
A program may use at most 64 MiB of HBM per device.

```python
import jax
import jax.numpy as jnp
from jax import lax

BS = 64
PCOL = 256
CLUSTERS = 1024
SLOTS = 64
N_GRID = 256
N_LAYER = 4


def draw_a_inner(key, part):
    key = jax.random.fold_in(key, 11)
    keys = jax.random.split(key, CLUSTERS * N_LAYER)
    chosen = jax.vmap(lambda single: jax.random.permutation(single, N_GRID))(keys)[:, :SLOTS]
    ordered = jnp.sort(chosen, axis=1)
    return ordered.reshape(CLUSTERS, N_LAYER, SLOTS).astype(jnp.int32)


def draw_a_count(key, part):
    key = jax.random.fold_in(key, 23)
    first_key, second_key = jax.random.split(key)
    counts = jax.random.randint(first_key, (CLUSTERS * N_LAYER,), SLOTS // 4, SLOTS + 1)
    where_full = jax.random.randint(second_key, (), 0, CLUSTERS * N_LAYER)
    positions = jnp.arange(CLUSTERS * N_LAYER)
    counts = jnp.where(positions == where_full, SLOTS, counts)
    return counts.reshape(CLUSTERS, N_LAYER).astype(jnp.int32)


def levels(key, extent, shards, low, top_value):
    def one(position, shards_of):
        steps = jax.random.uniform(jax.random.fold_in(jax.random.fold_in(key, 6), position), (shards_of,), jnp.float32, low / len(shards), top_value / len(shards))
        return jnp.repeat(jnp.exp(steps), extent[position] // shards_of).reshape((-1,) + (1,) * (len(extent) - position - 1))

    gain = one(*shards[0])
    for cut in shards[1:]:
        gain = gain * one(*cut)
    return gain


def bell_draw(key, shape, spread, reach, shards=(), kind=jnp.bfloat16):
    factor_of = levels(key, shape, shards, -0.22, 0.18) if shards else 1.0
    drawn = jax.random.normal(key, shape, jnp.float32) * spread * factor_of
    return jnp.minimum(jnp.maximum(drawn, -reach), reach).astype(kind)


def setup_inputs(seed: int = 0) -> dict:
    arg_keys = jax.random.split(jax.random.key(seed), 6)
    x_panel = bell_draw(arg_keys[0], (CLUSTERS * BS, PCOL), 1.0, 6.0, ((0, 1024),))
    b_panel = bell_draw(arg_keys[1], (CLUSTERS * BS, PCOL), 1.0, 6.0, ((0, 1024),))
    a_blocks = bell_draw(arg_keys[2], (CLUSTERS, N_LAYER, SLOTS, BS, BS), (N_LAYER * SLOTS * BS) ** -0.5, 0.046875, ((0, 256), (1, 4)))
    a_inner = draw_a_inner(jax.random.fold_in(arg_keys[5], 71), 0)
    a_count = draw_a_count(jax.random.fold_in(arg_keys[5], 71), 0)
    return {"x_panel": x_panel, "b_panel": b_panel, "a_blocks": a_blocks, "a_inner": a_inner, "a_count": a_count}


def reference(x_panel, b_panel, a_blocks, a_inner, a_count):
    grouped = b_panel.reshape(CLUSTERS, BS, PCOL)
    layer_ids = jnp.arange(N_LAYER, dtype=jnp.int32)[:, None]
    slot_ids = jnp.arange(SLOTS, dtype=jnp.int32)[None, :]

    def one_cluster(item):
        blocks, inner, count = item
        cluster = (inner * N_LAYER + layer_ids).astype(jnp.int32)
        chosen = grouped[cluster]
        live_mask = slot_ids < count[:, None]
        chosen = jnp.where(live_mask[:, :, None, None], chosen, jnp.zeros_like(chosen))
        partial_value = jnp.einsum("lsij,lsjc->lic", blocks.astype(jnp.float32), chosen.astype(jnp.float32))
        return jnp.sum(partial_value, axis=0)

    product = lax.map(one_cluster, (a_blocks, a_inner, a_count))
    product = product.reshape(CLUSTERS * BS, PCOL)
    return (1.5 * x_panel.astype(jnp.float32) - 0.5 * product).astype(jnp.bfloat16)
```

```python
import functools

import jax
import jax.numpy as jnp
import numpy as np
from jax import lax
from jax.experimental import pallas as pl
from jax.experimental.pallas import tpu as pltpu
from jax.sharding import Mesh
from jax.sharding import PartitionSpec as P

NEAR = 4
NZF, NYF, NXH, NXL, NC = 4, 2, 2, 2, 2
NZ, NY = NZF * NEAR, NYF * NEAR
Z, Y = ("zf", "zn"), ("yf", "yn")
AXES = Z + Y + ("xh", "xl", "c")
DIMS = (NZF, NEAR, NYF, NEAR, NXH, NXL, NC)
BS = 64
HALF = 128
WIDE = 256
PER_TILE = WIDE // BS
CLUSTERS = 256
TILES = CLUSTERS // PER_TILE
STEP_TILES = 8
MIB = 1024 * 1024


def pack_kernel(index_ref, a_ref, out_ref):
    pairs = a_ref.shape[2] // 2
    for pair in range(pairs):
        out_ref[0, pair] = jnp.concatenate([a_ref[0, 0, 2 * pair], a_ref[0, 0, 2 * pair + 1]], axis=-1)
    index = index_ref[0].astype(jnp.float32)
    out_ref[0, pairs] = jnp.broadcast_to(jnp.concatenate([index, index], axis=-1), (BS, 2 * BS)).astype(out_ref.dtype)


def pack(a_blocks, masked):
    rows, _, slots, bs, _ = a_blocks.shape
    return pl.pallas_call(
        pack_kernel,
        grid=(rows,),
        in_specs=[
            pl.BlockSpec((1, 1, slots), lambda r: (r, 0, 0)),
            pl.BlockSpec((1, 1, slots, bs, bs), lambda r: (r, 0, 0, 0, 0)),
        ],
        out_specs=pl.BlockSpec((1, slots // 2 + 1, bs, 2 * bs), lambda r: (r, 0, 0, 0)),
        out_shape=jax.ShapeDtypeStruct((rows, slots // 2 + 1, bs, 2 * bs), a_blocks.dtype),
        cost_estimate=pl.CostEstimate(flops=0, bytes_accessed=6 * MIB, transcendentals=0),
        compiler_params=pltpu.CompilerParams(vmem_limit_bytes=8 * MIB),
    )(masked, a_blocks)


def spread_kernel(pos_ref, packed_ref, out_ref):
    row = pl.program_id(0)
    lane = lax.broadcasted_iota(jnp.int32, (BS, 2 * BS), 1)
    out_ref[...] = jnp.zeros_like(out_ref)

    def one_pair(pair, carry):
        straight = packed_ref[0, pair]
        swapped = jnp.concatenate([straight[:, BS:], straight[:, :BS]], axis=-1)
        for side in range(2):
            pos = pos_ref[row, 2 * pair + side]
            tile = pos // PER_TILE
            within = pos % PER_TILE
            at = pl.ds(pl.multiple_of((within // 2) * (2 * BS), 2 * BS), 2 * BS)
            to_side = within % 2
            value = jnp.where(to_side == side, straight, swapped)
            mine = (lane >= BS) == (to_side == 1)
            out_ref[tile, :, at] = jnp.where(mine, value, out_ref[tile, :, at])
        return carry

    lax.fori_loop(0, packed_ref.shape[1], one_pair, 0, unroll=4)


def spread(packed, pos):
    rows, more, bs, wide = packed.shape
    return pl.pallas_call(
        spread_kernel,
        grid_spec=pltpu.PrefetchScalarGridSpec(
            num_scalar_prefetch=1,
            grid=(rows,),
            in_specs=[pl.BlockSpec((1, more - 1, bs, wide), lambda r, pos: (r, 0, 0, 0))],
            out_specs=pl.BlockSpec((TILES + 1, bs, WIDE), lambda r, pos: (0, r, 0)),
        ),
        out_shape=jax.ShapeDtypeStruct((TILES + 1, rows * bs, WIDE), packed.dtype),
        cost_estimate=pl.CostEstimate(flops=0, bytes_accessed=20 * MIB, transcendentals=0),
        compiler_params=pltpu.CompilerParams(vmem_limit_bytes=8 * MIB),
    )(pos, packed)


def multiply_kernel(has_acc, own_ref, other_ref, b_ref, *rest):
    out_ref = rest[-1]
    rows = own_ref.shape[1]

    @pl.when(pl.program_id(0) == 0)
    def _():
        out_ref[...] = rest[0][...] if has_acc else jnp.zeros_like(out_ref)

    for half, ref in enumerate((own_ref, other_ref)):
        total = out_ref[half]
        for t in range(ref.shape[0]):
            total = total + jnp.dot(ref[t], b_ref[t * WIDE : (t + 1) * WIDE, :], preferred_element_type=jnp.float32)
        out_ref[half] = total


def multiply(own, other, piece, first, acc):
    rows = own.shape[1]
    count = piece.shape[0] // WIDE
    step = min(STEP_TILES, count)
    base = first // (PER_TILE * step)
    a_spec = pl.BlockSpec((step, rows, WIDE), lambda i: (base + i, 0, 0))
    acc_spec = pl.BlockSpec((2, rows, HALF), lambda i: (0, 0, 0))
    extra = [] if acc is None else [acc]
    return pl.pallas_call(
        functools.partial(multiply_kernel, acc is not None),
        grid=(count // step,),
        in_specs=[a_spec, a_spec, pl.BlockSpec((step * WIDE, HALF), lambda i: (i, 0))] + [acc_spec] * len(extra),
        out_specs=acc_spec,
        out_shape=jax.ShapeDtypeStruct((2, rows, HALF), jnp.float32),
        cost_estimate=pl.CostEstimate(
            flops=2 * 2 * rows * HALF * piece.shape[0], bytes_accessed=2 * rows * piece.shape[0] * 2, transcendentals=0
        ),
        compiler_params=pltpu.CompilerParams(vmem_limit_bytes=8 * MIB),
    )(own, other, piece, *extra)


def near_pairs(stage, by):
    ids = np.arange(np.prod(DIMS)).reshape(DIMS)
    pairs = []
    for core in range(NC):
        along_z = core == stage
        grid = ids[..., core].reshape((NZ, NY) + DIMS[4:6])
        moved = np.roll(grid, -by, axis=0 if along_z else 1)
        pairs += list(zip(grid.ravel().tolist(), moved.ravel().tolist()))
    return sorted(pairs)


def near_shift(x, stage, by):
    return lax.ppermute(x, AXES, near_pairs(stage, by))


def gather_near(x, stage):
    h = x.shape[0] // 2
    first, second, x = lax.optimization_barrier((x[:h], x[h:], x))
    minus, plus = near_shift(x, stage, 1), near_shift(x, stage, -1)
    return minus, plus, near_shift(first, stage, 2), near_shift(second, stage, -2)


def place_of(delta, low):
    w = (delta + low) % NEAR - low
    return jnp.where(w == 0, 0, jnp.where(w == -1, 1, jnp.where(w == 1, 2, 3)))


def positions(masked):
    q = masked
    z, y, xh = q // (NY * NXH), (q // NXH) % NY, q % NXH
    low = 2 - xh
    by_z = place_of((z - lax.axis_index(Z)) % NZ, low)
    by_y = place_of((y - lax.axis_index(Y)) % NY, low)
    core = lax.axis_index("c")
    first = jnp.where(core == 0, by_z, by_y)
    second = jnp.where(core == 0, by_y, by_z)
    pos = second * 64 + xh * 32 + first * 8 + (z // NEAR) * NYF + y // NEAR
    return jnp.where(q < CLUSTERS, pos, CLUSTERS).astype(jnp.int32)


def per_device(x_panel, b_panel, a_blocks, a_inner, a_count):
    rows, _, slots, bs, _ = a_blocks.shape
    xh = lax.axis_index("xh")
    live = lax.broadcasted_iota(jnp.int32, a_inner.shape, 2) < a_count[:, :, None]
    masked = jnp.where(live, a_inner, CLUSTERS)

    far = NZF * NYF
    sent = jnp.concatenate(
        [jnp.broadcast_to(b_panel[None, :, h * HALF : (h + 1) * HALF], (far, bs, HALF)) for h in range(NXH)]
    )
    packed = pack(a_blocks, masked)
    sent, packed = lax.optimization_barrier((sent, packed))
    packed_other = lax.ppermute(packed, "xh", [(0, 1), (1, 0)])
    block = lax.all_to_all(sent, ("xh", "zf", "yf"), 0, 0, tiled=False).reshape(-1, HALF)
    own = spread(packed, positions(masked[:, 0, :]))

    block, own = lax.optimization_barrier((block, own))
    h = block.shape[0] // 2
    minus, plus, first, second = gather_near(block, 0)
    plane = jnp.concatenate(
        [block[:h], minus[:h], plus[:h], first, block[h:], minus[h:], plus[h:], second]
    )
    plane, packed_other = lax.optimization_barrier((plane, packed_other))
    pieces = gather_near(plane, 1)

    masked_other = packed_other[:, slots // 2, 0, :slots].astype(jnp.int32)
    other = spread(packed_other, positions(masked_other))
    acc = multiply(own, other, plane, 0, None)
    for piece, at in zip(pieces, (64, 128, 192, 224)):
        acc = multiply(own, other, piece, at, acc)

    ordered = jnp.where(xh == 0, acc, acc[::-1])
    back = lax.all_to_all(ordered.reshape(NXH * rows, bs, HALF), ("xh", "xl", "c"), 0, 0, tiled=False)
    halves = back.reshape(NXH, NXL * NC, bs, HALF).sum(axis=1)
    product = jnp.concatenate([halves[0], halves[1]], axis=-1)
    return (1.5 * x_panel.astype(jnp.float32) - 0.5 * product).astype(jnp.bfloat16)


def solution(mesh):
    fine = Mesh(mesh.devices.reshape(DIMS), AXES)
    grid, layer = Z + Y + ("xh",), ("xl", "c")
    placed = (
        P(grid + layer, None),
        P(grid + layer, None),
        P(grid, layer, None, None, None),
        P(grid, layer, None),
        P(grid, layer),
    )
    return jax.shard_map(
        per_device,
        mesh=fine,
        in_specs=placed,
        out_specs=P(grid + layer, None),
        check_vma=False,
    )
```

```python
import functools

import jax
import jax.numpy as jnp
import numpy as np
from jax import lax
from jax.experimental import pallas as pl
from jax.experimental.pallas import tpu as pltpu
from jax.sharding import Mesh
from jax.sharding import PartitionSpec as P

NEAR = 4
NZF, NYF, NXH, NXL, NC = 4, 2, 2, 2, 2
NZ, NY = NZF * NEAR, NYF * NEAR
Z, Y = ("zf", "zn"), ("yf", "yn")
AXES = Z + Y + ("xh", "xl", "c")
DIMS = (NZF, NEAR, NYF, NEAR, NXH, NXL, NC)
BS = 64
HALF = 128
WIDE = 256
PER_TILE = WIDE // BS
CLUSTERS = 256
TILES = CLUSTERS // PER_TILE
STEP_TILES = 8
MIB = 1024 * 1024


def pack_kernel(index_ref, a_ref, out_ref):
    pairs = a_ref.shape[2] // 2
    for pair in range(pairs):
        out_ref[0, pair] = jnp.concatenate([a_ref[0, 0, 2 * pair], a_ref[0, 0, 2 * pair + 1]], axis=-1)
    index = index_ref[0].astype(jnp.float32)
    out_ref[0, pairs] = jnp.broadcast_to(jnp.concatenate([index, index], axis=-1), (BS, 2 * BS)).astype(out_ref.dtype)


def pack(a_blocks, masked, first, rows):
    _, _, slots, bs, _ = a_blocks.shape
    return pl.pallas_call(
        pack_kernel,
        grid=(rows,),
        in_specs=[
            pl.BlockSpec((1, 1, slots), lambda r: (first + r, 0, 0)),
            pl.BlockSpec((1, 1, slots, bs, bs), lambda r: (first + r, 0, 0, 0, 0)),
        ],
        out_specs=pl.BlockSpec((1, slots // 2 + 1, bs, 2 * bs), lambda r: (r, 0, 0, 0)),
        out_shape=jax.ShapeDtypeStruct((rows, slots // 2 + 1, bs, 2 * bs), a_blocks.dtype),
        cost_estimate=pl.CostEstimate(flops=0, bytes_accessed=6 * MIB, transcendentals=0),
        compiler_params=pltpu.CompilerParams(vmem_limit_bytes=8 * MIB),
    )(masked, a_blocks)


def spread_kernel(split, pos_ref, low_ref, high_ref, out_ref):
    row = pl.program_id(0)
    lane = lax.broadcasted_iota(jnp.int32, (BS, 2 * BS), 1)
    out_ref[...] = jnp.zeros_like(out_ref)

    def place(packed_ref):
        def one_pair(pair, carry):
            straight = packed_ref[0, pair]
            swapped = jnp.concatenate([straight[:, BS:], straight[:, :BS]], axis=-1)
            for side in range(2):
                pos = pos_ref[row, 2 * pair + side]
                tile = pos // PER_TILE
                within = pos % PER_TILE
                at = pl.ds(pl.multiple_of((within // 2) * (2 * BS), 2 * BS), 2 * BS)
                to_side = within % 2
                value = jnp.where(to_side == side, straight, swapped)
                mine = (lane >= BS) == (to_side == 1)
                out_ref[tile, :, at] = jnp.where(mine, value, out_ref[tile, :, at])
            return carry

        lax.fori_loop(0, packed_ref.shape[1], one_pair, 0, unroll=4)

    pl.when(row < split)(lambda: place(low_ref))
    pl.when(row >= split)(lambda: place(high_ref))


def spread(low, high, pos):
    split, more, bs, wide = low.shape
    rows = split + high.shape[0]
    return pl.pallas_call(
        functools.partial(spread_kernel, split),
        grid_spec=pltpu.PrefetchScalarGridSpec(
            num_scalar_prefetch=1,
            grid=(rows,),
            in_specs=[
                pl.BlockSpec((1, more - 1, bs, wide), lambda r, pos: (jnp.minimum(r, split - 1), 0, 0, 0)),
                pl.BlockSpec((1, more - 1, bs, wide), lambda r, pos: (jnp.maximum(r - split, 0), 0, 0, 0)),
            ],
            out_specs=pl.BlockSpec((TILES + 1, bs, WIDE), lambda r, pos: (0, r, 0)),
        ),
        out_shape=jax.ShapeDtypeStruct((TILES + 1, rows * bs, WIDE), low.dtype),
        cost_estimate=pl.CostEstimate(flops=0, bytes_accessed=20 * MIB, transcendentals=0),
        compiler_params=pltpu.CompilerParams(vmem_limit_bytes=9 * MIB),
    )(pos, low, high)


def multiply_kernel(has_acc, own_ref, other_ref, b_ref, *rest):
    out_ref = rest[-1]
    rows = own_ref.shape[1]

    @pl.when(pl.program_id(0) == 0)
    def _():
        out_ref[...] = rest[0][...] if has_acc else jnp.zeros_like(out_ref)

    for half, ref in enumerate((own_ref, other_ref)):
        total = out_ref[half]
        for t in range(ref.shape[0]):
            total = total + jnp.dot(ref[t], b_ref[t * WIDE : (t + 1) * WIDE, :], preferred_element_type=jnp.float32)
        out_ref[half] = total


def multiply(own, other, piece, first, acc):
    rows = own.shape[1]
    count = piece.shape[0] // WIDE
    step = min(STEP_TILES, count)
    base = first // (PER_TILE * step)
    a_spec = pl.BlockSpec((step, rows, WIDE), lambda i: (base + i, 0, 0))
    acc_spec = pl.BlockSpec((2, rows, HALF), lambda i: (0, 0, 0))
    extra = [] if acc is None else [acc]
    return pl.pallas_call(
        functools.partial(multiply_kernel, acc is not None),
        grid=(count // step,),
        in_specs=[a_spec, a_spec, pl.BlockSpec((step * WIDE, HALF), lambda i: (i, 0))] + [acc_spec] * len(extra),
        out_specs=acc_spec,
        out_shape=jax.ShapeDtypeStruct((2, rows, HALF), jnp.float32),
        cost_estimate=pl.CostEstimate(
            flops=2 * 2 * rows * HALF * piece.shape[0], bytes_accessed=2 * rows * piece.shape[0] * 2, transcendentals=0
        ),
        compiler_params=pltpu.CompilerParams(vmem_limit_bytes=8 * MIB),
    )(own, other, piece, *extra)


def near_pairs(stage, by):
    ids = np.arange(np.prod(DIMS)).reshape(DIMS)
    pairs = []
    for core in range(NC):
        along_z = core == stage
        grid = ids[..., core].reshape((NZ, NY) + DIMS[4:6])
        moved = np.roll(grid, -by, axis=0 if along_z else 1)
        pairs += list(zip(grid.ravel().tolist(), moved.ravel().tolist()))
    return sorted(pairs)


def near_shift(x, stage, by):
    return lax.ppermute(x, AXES, near_pairs(stage, by))


def gather_near(x, stage, beside=()):
    h = x.shape[0] // 2
    first, second, x = lax.optimization_barrier((x[:h], x[h:], x))
    minus, plus, first = near_shift(x, stage, 1), near_shift(x, stage, -1), near_shift(first, stage, 2)
    second, *beside = lax.optimization_barrier((second, *beside))
    return (minus, plus, first, near_shift(second, stage, -2)), beside


def place_of(delta, low):
    w = (delta + low) % NEAR - low
    return jnp.where(w == 0, 0, jnp.where(w == -1, 1, jnp.where(w == 1, 2, 3)))


def positions(masked):
    q = masked
    z, y, xh = q // (NY * NXH), (q // NXH) % NY, q % NXH
    zf, yf = z // NEAR, y // NEAR
    part = zf // 2
    low = 2 - part
    by_z = place_of((z - lax.axis_index(Z)) % NZ, low)
    by_y = place_of((y - lax.axis_index(Y)) % NY, low)
    core = lax.axis_index("c")
    first = jnp.where(core == 0, by_z, by_y)
    second = jnp.where(core == 0, by_y, by_z)
    pos = second * 64 + part * 32 + first * 8 + (zf % 2) * 4 + yf * NXH + xh
    return jnp.where(q < CLUSTERS, pos, CLUSTERS).astype(jnp.int32)


def per_device(x_panel, b_panel, a_blocks, a_inner, a_count):
    rows, _, slots, bs, _ = a_blocks.shape
    xh = lax.axis_index("xh")
    live = lax.broadcasted_iota(jnp.int32, a_inner.shape, 2) < a_count[:, :, None]
    masked = jnp.where(live, a_inner, CLUSTERS)

    left, right = b_panel[:, :HALF], b_panel[:, HALF:]
    got = lax.ppermute(jnp.where(xh == 0, right, left), "xh", [(0, 1), (1, 0)])
    mine = jnp.where(xh == 0, left, right)
    pair = jnp.where(xh == 0, jnp.concatenate([mine, got]), jnp.concatenate([got, mine]))
    split = rows // 2
    low, high = pack(a_blocks, masked, 0, split), pack(a_blocks, masked, split, rows - split)
    pair, low, high = lax.optimization_barrier((pair, low, high))
    low_other = lax.ppermute(low, "xh", [(0, 1), (1, 0)])
    sent = jnp.broadcast_to(pair[None], (NZF * NYF,) + pair.shape)
    block = lax.all_to_all(sent, ("zf", "yf"), 0, 0, tiled=False).reshape(-1, HALF)
    own = spread(low, high, positions(masked[:, 0, :]))

    block, own = lax.optimization_barrier((block, own))
    h = block.shape[0] // 2
    (minus, plus, first, second), (low_other, high) = gather_near(block, 0, (low_other, high))
    high_other = lax.ppermute(high, "xh", [(0, 1), (1, 0)])
    plane = jnp.concatenate(
        [block[:h], minus[:h], plus[:h], first, block[h:], minus[h:], plus[h:], second]
    )
    pieces, _ = gather_near(plane, 1)

    masked_other = jnp.concatenate([p[:, slots // 2, 0, :slots] for p in (low_other, high_other)]).astype(jnp.int32)
    other = spread(low_other, high_other, positions(masked_other))
    acc = multiply(own, other, plane, 0, None)
    for piece, at in zip(pieces, (64, 128, 192, 224)):
        acc = multiply(own, other, piece, at, acc)

    ordered = jnp.where(xh == 0, acc, acc[::-1])
    back = lax.all_to_all(ordered.reshape(NXH * rows, bs, HALF), ("xh", "xl", "c"), 0, 0, tiled=False)
    halves = back.reshape(NXH, NXL * NC, bs, HALF).sum(axis=1)
    product = jnp.concatenate([halves[0], halves[1]], axis=-1)
    return (1.5 * x_panel.astype(jnp.float32) - 0.5 * product).astype(jnp.bfloat16)


def solution(mesh):
    fine = Mesh(mesh.devices.reshape(DIMS), AXES)
    grid, layer = Z + Y + ("xh",), ("xl", "c")
    placed = (
        P(grid + layer, None),
        P(grid + layer, None),
        P(grid, layer, None, None, None),
        P(grid, layer, None),
        P(grid, layer),
    )
    return jax.shard_map(
        per_device,
        mesh=fine,
        in_specs=placed,
        out_specs=P(grid + layer, None),
        check_vma=False,
    )
```

```python
import functools

import jax
import jax.numpy as jnp
import numpy as np
from jax import lax
from jax.experimental import pallas as pl
from jax.experimental.pallas import tpu as pltpu
from jax.sharding import Mesh
from jax.sharding import PartitionSpec as P

NEAR = 4
NZF, NYF, NXH, NXL, NC = 4, 2, 2, 2, 2
NZ, NY = NZF * NEAR, NYF * NEAR
Z, Y = ("zf", "zn"), ("yf", "yn")
AXES = Z + Y + ("xh", "xl", "c")
DIMS = (NZF, NEAR, NYF, NEAR, NXH, NXL, NC)
BS = 64
HALF = 128
WIDE = 256
PER_TILE = WIDE // BS
CLUSTERS = 256
TILES = CLUSTERS // PER_TILE
STEP_TILES = 8
MIB = 1024 * 1024


def pack_kernel(index_ref, a_ref, out_ref):
    pairs = a_ref.shape[2] // 2
    for pair in range(pairs):
        out_ref[0, pair] = jnp.concatenate([a_ref[0, 0, 2 * pair], a_ref[0, 0, 2 * pair + 1]], axis=-1)
    index = index_ref[0].astype(jnp.float32)
    out_ref[0, pairs] = jnp.broadcast_to(jnp.concatenate([index, index], axis=-1), (BS, 2 * BS)).astype(out_ref.dtype)


def pack(a_blocks, masked, first, rows):
    _, _, slots, bs, _ = a_blocks.shape
    return pl.pallas_call(
        pack_kernel,
        grid=(rows,),
        in_specs=[
            pl.BlockSpec((1, 1, slots), lambda r: (first + r, 0, 0)),
            pl.BlockSpec((1, 1, slots, bs, bs), lambda r: (first + r, 0, 0, 0, 0)),
        ],
        out_specs=pl.BlockSpec((1, slots // 2 + 1, bs, 2 * bs), lambda r: (r, 0, 0, 0)),
        out_shape=jax.ShapeDtypeStruct((rows, slots // 2 + 1, bs, 2 * bs), a_blocks.dtype),
        cost_estimate=pl.CostEstimate(flops=0, bytes_accessed=6 * MIB, transcendentals=0),
        compiler_params=pltpu.CompilerParams(vmem_limit_bytes=8 * MIB),
    )(masked, a_blocks)


def spread_kernel(first, pos_ref, packed_ref, *rest):
    out_ref = rest[-1]
    row = first + pl.program_id(0)
    lane = lax.broadcasted_iota(jnp.int32, (BS, 2 * BS), 1)
    out_ref[...] = jnp.zeros_like(out_ref)

    def one_pair(pair, carry):
        straight = packed_ref[0, pair]
        swapped = jnp.concatenate([straight[:, BS:], straight[:, :BS]], axis=-1)
        for side in range(2):
            pos = pos_ref[row, 2 * pair + side]
            tile = pos // PER_TILE
            within = pos % PER_TILE
            at = pl.ds(pl.multiple_of((within // 2) * (2 * BS), 2 * BS), 2 * BS)
            to_side = within % 2
            value = jnp.where(to_side == side, straight, swapped)
            mine = (lane >= BS) == (to_side == 1)
            out_ref[tile, :, at] = jnp.where(mine, value, out_ref[tile, :, at])
        return carry

    lax.fori_loop(0, packed_ref.shape[1], one_pair, 0, unroll=4)


def spread(packed, pos, first, rows, into=None):
    here, more, bs, wide = packed.shape
    extra = [] if into is None else [into]
    return pl.pallas_call(
        functools.partial(spread_kernel, first),
        grid_spec=pltpu.PrefetchScalarGridSpec(
            num_scalar_prefetch=1,
            grid=(here,),
            in_specs=[pl.BlockSpec((1, more - 1, bs, wide), lambda r, pos: (r, 0, 0, 0))]
            + [pl.BlockSpec(memory_space=pl.ANY)] * len(extra),
            out_specs=pl.BlockSpec((TILES + 1, bs, WIDE), lambda r, pos: (0, first + r, 0)),
        ),
        out_shape=jax.ShapeDtypeStruct((TILES + 1, rows * bs, WIDE), packed.dtype),
        input_output_aliases={2: 0} if extra else {},
        cost_estimate=pl.CostEstimate(flops=0, bytes_accessed=10 * MIB, transcendentals=0),
        compiler_params=pltpu.CompilerParams(vmem_limit_bytes=8 * MIB),
    )(pos, packed, *extra)


def multiply_kernel(has_acc, own_ref, other_ref, b_ref, *rest):
    out_ref = rest[-1]
    rows = own_ref.shape[1]

    @pl.when(pl.program_id(0) == 0)
    def _():
        out_ref[...] = rest[0][...] if has_acc else jnp.zeros_like(out_ref)

    for half, ref in enumerate((own_ref, other_ref)):
        total = out_ref[half]
        for t in range(ref.shape[0]):
            total = total + jnp.dot(ref[t], b_ref[t * WIDE : (t + 1) * WIDE, :], preferred_element_type=jnp.float32)
        out_ref[half] = total


def multiply(own, other, piece, first, acc):
    rows = own.shape[1]
    count = piece.shape[0] // WIDE
    step = min(STEP_TILES, count)
    base = first // (PER_TILE * step)
    a_spec = pl.BlockSpec((step, rows, WIDE), lambda i: (base + i, 0, 0))
    acc_spec = pl.BlockSpec((2, rows, HALF), lambda i: (0, 0, 0))
    extra = [] if acc is None else [acc]
    return pl.pallas_call(
        functools.partial(multiply_kernel, acc is not None),
        grid=(count // step,),
        in_specs=[a_spec, a_spec, pl.BlockSpec((step * WIDE, HALF), lambda i: (i, 0))] + [acc_spec] * len(extra),
        out_specs=acc_spec,
        out_shape=jax.ShapeDtypeStruct((2, rows, HALF), jnp.float32),
        cost_estimate=pl.CostEstimate(
            flops=2 * 2 * rows * HALF * piece.shape[0], bytes_accessed=2 * rows * piece.shape[0] * 2, transcendentals=0
        ),
        compiler_params=pltpu.CompilerParams(vmem_limit_bytes=8 * MIB),
    )(own, other, piece, *extra)


def near_pairs(stage, by):
    ids = np.arange(np.prod(DIMS)).reshape(DIMS)
    pairs = []
    for core in range(NC):
        along_z = core == stage
        grid = ids[..., core].reshape((NZ, NY) + DIMS[4:6])
        moved = np.roll(grid, -by, axis=0 if along_z else 1)
        pairs += list(zip(grid.ravel().tolist(), moved.ravel().tolist()))
    return sorted(pairs)


def near_shift(x, stage, by):
    return lax.ppermute(x, AXES, near_pairs(stage, by))


def gather_near(x, stage, beside=()):
    h = x.shape[0] // 2
    first, second, x = lax.optimization_barrier((x[:h], x[h:], x))
    minus, plus, first = near_shift(x, stage, 1), near_shift(x, stage, -1), near_shift(first, stage, 2)
    second, *beside = lax.optimization_barrier((second, *beside))
    return (minus, plus, first, near_shift(second, stage, -2)), beside


def place_of(delta, low):
    w = (delta + low) % NEAR - low
    return jnp.where(w == 0, 0, jnp.where(w == -1, 1, jnp.where(w == 1, 2, 3)))


def positions(masked):
    q = masked
    z, y, xh = q // (NY * NXH), (q // NXH) % NY, q % NXH
    zf, yf = z // NEAR, y // NEAR
    part = zf // 2
    low = 2 - part
    by_z = place_of((z - lax.axis_index(Z)) % NZ, low)
    by_y = place_of((y - lax.axis_index(Y)) % NY, low)
    core = lax.axis_index("c")
    first = jnp.where(core == 0, by_z, by_y)
    second = jnp.where(core == 0, by_y, by_z)
    pos = second * 64 + part * 32 + first * 8 + (zf % 2) * 4 + yf * NXH + xh
    return jnp.where(q < CLUSTERS, pos, CLUSTERS).astype(jnp.int32)


def per_device(x_panel, b_panel, a_blocks, a_inner, a_count):
    rows, _, slots, bs, _ = a_blocks.shape
    xh = lax.axis_index("xh")
    live = lax.broadcasted_iota(jnp.int32, a_inner.shape, 2) < a_count[:, :, None]
    masked = jnp.where(live, a_inner, CLUSTERS)

    left, right = b_panel[:, :HALF], b_panel[:, HALF:]
    got = lax.ppermute(jnp.where(xh == 0, right, left), "xh", [(0, 1), (1, 0)])
    mine = jnp.where(xh == 0, left, right)
    pair = jnp.where(xh == 0, jnp.concatenate([mine, got]), jnp.concatenate([got, mine]))
    split = rows // 2
    low, high = pack(a_blocks, masked, 0, split), pack(a_blocks, masked, split, rows - split)
    low_other = lax.ppermute(low, "xh", [(0, 1), (1, 0)])
    sent = jnp.broadcast_to(pair[None], (NZF * NYF,) + pair.shape)
    block = lax.all_to_all(sent, ("zf", "yf"), 0, 0, tiled=False).reshape(-1, HALF)
    own_pos = positions(masked[:, 0, :])
    own = spread(high, own_pos, split, rows, spread(low, own_pos, 0, rows))

    block, own = lax.optimization_barrier((block, own))
    h = block.shape[0] // 2
    (minus, plus, first, second), (low_other, high) = gather_near(block, 0, (low_other, high))
    high_other = lax.ppermute(high, "xh", [(0, 1), (1, 0)])
    plane = jnp.concatenate(
        [block[:h], minus[:h], plus[:h], first, block[h:], minus[h:], plus[h:], second]
    )
    pieces, _ = gather_near(plane, 1)
    arrived, low_other = lax.optimization_barrier((pieces[0], low_other))
    pieces = (arrived,) + pieces[1:]

    def positions_in(p):
        return positions(p[:, slots // 2, 0, :slots].astype(jnp.int32))

    other = spread(low_other, positions_in(low_other), 0, rows)
    late = jnp.pad(positions_in(high_other), ((split, 0), (0, 0)))
    other = spread(high_other, late, split, rows, other)
    acc = multiply(own, other, plane, 0, None)
    for piece, at in zip(pieces, (64, 128, 192, 224)):
        acc = multiply(own, other, piece, at, acc)

    ordered = jnp.where(xh == 0, acc, acc[::-1])
    back = lax.all_to_all(ordered.reshape(NXH * rows, bs, HALF), ("xh", "xl", "c"), 0, 0, tiled=False)
    halves = back.reshape(NXH, NXL * NC, bs, HALF).sum(axis=1)
    product = jnp.concatenate([halves[0], halves[1]], axis=-1)
    return (1.5 * x_panel.astype(jnp.float32) - 0.5 * product).astype(jnp.bfloat16)


def solution(mesh):
    fine = Mesh(mesh.devices.reshape(DIMS), AXES)
    grid, layer = Z + Y + ("xh",), ("xl", "c")
    placed = (
        P(grid + layer, None),
        P(grid + layer, None),
        P(grid, layer, None, None, None),
        P(grid, layer, None),
        P(grid, layer),
    )
    return jax.shard_map(
        per_device,
        mesh=fine,
        in_specs=placed,
        out_specs=P(grid + layer, None),
        check_vma=False,
    )
```

```python
import functools

import jax
import jax.numpy as jnp
import numpy as np
from jax import lax
from jax.experimental import pallas as pl
from jax.experimental.pallas import tpu as pltpu
from jax.sharding import Mesh
from jax.sharding import PartitionSpec as P

NEAR = 4
NZF, NYF, NXH, NXL, NC = 4, 2, 2, 2, 2
NZ, NY = NZF * NEAR, NYF * NEAR
Z, Y = ("zf", "zn"), ("yf", "yn")
AXES = Z + Y + ("xh", "xl", "c")
DIMS = (NZF, NEAR, NYF, NEAR, NXH, NXL, NC)
BS = 64
HALF = 128
WIDE = 256
PER_TILE = WIDE // BS
CLUSTERS = 256
TILES = CLUSTERS // PER_TILE
STEP_TILES = 8
MIB = 1024 * 1024


def pack_kernel(index_ref, a_ref, out_ref):
    pairs = a_ref.shape[2] // 2
    for pair in range(pairs):
        out_ref[0, pair] = jnp.concatenate([a_ref[0, 0, 2 * pair], a_ref[0, 0, 2 * pair + 1]], axis=-1)
    index = index_ref[0].astype(jnp.float32)
    out_ref[0, pairs] = jnp.broadcast_to(jnp.concatenate([index, index], axis=-1), (BS, 2 * BS)).astype(out_ref.dtype)


def pack(a_blocks, masked, first, rows):
    _, _, slots, bs, _ = a_blocks.shape
    return pl.pallas_call(
        pack_kernel,
        grid=(rows,),
        in_specs=[
            pl.BlockSpec((1, 1, slots), lambda r: (first + r, 0, 0)),
            pl.BlockSpec((1, 1, slots, bs, bs), lambda r: (first + r, 0, 0, 0, 0)),
        ],
        out_specs=pl.BlockSpec((1, slots // 2 + 1, bs, 2 * bs), lambda r: (r, 0, 0, 0)),
        out_shape=jax.ShapeDtypeStruct((rows, slots // 2 + 1, bs, 2 * bs), a_blocks.dtype),
        cost_estimate=pl.CostEstimate(flops=0, bytes_accessed=6 * MIB, transcendentals=0),
        compiler_params=pltpu.CompilerParams(vmem_limit_bytes=8 * MIB),
    )(masked, a_blocks)


def spread_kernel(split, pos_ref, low_ref, high_ref, out_ref):
    row = pl.program_id(0)
    lane = lax.broadcasted_iota(jnp.int32, (BS, 2 * BS), 1)
    out_ref[...] = jnp.zeros_like(out_ref)

    def place(packed_ref):
        def one_pair(pair, carry):
            straight = packed_ref[0, pair]
            swapped = jnp.concatenate([straight[:, BS:], straight[:, :BS]], axis=-1)
            for side in range(2):
                pos = pos_ref[row, 2 * pair + side]
                tile = pos // PER_TILE
                within = pos % PER_TILE
                at = pl.ds(pl.multiple_of((within // 2) * (2 * BS), 2 * BS), 2 * BS)
                to_side = within % 2
                value = jnp.where(to_side == side, straight, swapped)
                mine = (lane >= BS) == (to_side == 1)
                out_ref[tile, :, at] = jnp.where(mine, value, out_ref[tile, :, at])
            return carry

        lax.fori_loop(0, packed_ref.shape[1], one_pair, 0, unroll=4)

    pl.when(row < split)(lambda: place(low_ref))
    pl.when(row >= split)(lambda: place(high_ref))


def spread(low, high, pos):
    split, more, bs, wide = low.shape
    rows = split + high.shape[0]
    return pl.pallas_call(
        functools.partial(spread_kernel, split),
        grid_spec=pltpu.PrefetchScalarGridSpec(
            num_scalar_prefetch=1,
            grid=(rows,),
            in_specs=[
                pl.BlockSpec((1, more - 1, bs, wide), lambda r, pos: (jnp.minimum(r, split - 1), 0, 0, 0)),
                pl.BlockSpec((1, more - 1, bs, wide), lambda r, pos: (jnp.maximum(r - split, 0), 0, 0, 0)),
            ],
            out_specs=pl.BlockSpec((TILES + 1, bs, WIDE), lambda r, pos: (0, r, 0)),
        ),
        out_shape=jax.ShapeDtypeStruct((TILES + 1, rows * bs, WIDE), low.dtype),
        cost_estimate=pl.CostEstimate(flops=0, bytes_accessed=20 * MIB, transcendentals=0),
        compiler_params=pltpu.CompilerParams(vmem_limit_bytes=9 * MIB),
    )(pos, low, high)


def multiply_kernel(has_acc, own_ref, other_ref, b_ref, *rest):
    out_ref = rest[-1]
    rows = own_ref.shape[1]

    @pl.when(pl.program_id(0) == 0)
    def _():
        out_ref[...] = rest[0][...] if has_acc else jnp.zeros_like(out_ref)

    for half, ref in enumerate((own_ref, other_ref)):
        total = out_ref[half]
        for t in range(ref.shape[0]):
            total = total + jnp.dot(ref[t], b_ref[t * WIDE : (t + 1) * WIDE, :], preferred_element_type=jnp.float32)
        out_ref[half] = total


def multiply(own, other, piece, first, acc):
    rows = own.shape[1]
    count = piece.shape[0] // WIDE
    step = min(STEP_TILES, count)
    base = first // (PER_TILE * step)
    a_spec = pl.BlockSpec((step, rows, WIDE), lambda i: (base + i, 0, 0))
    acc_spec = pl.BlockSpec((2, rows, HALF), lambda i: (0, 0, 0))
    extra = [] if acc is None else [acc]
    return pl.pallas_call(
        functools.partial(multiply_kernel, acc is not None),
        grid=(count // step,),
        in_specs=[a_spec, a_spec, pl.BlockSpec((step * WIDE, HALF), lambda i: (i, 0))] + [acc_spec] * len(extra),
        out_specs=acc_spec,
        out_shape=jax.ShapeDtypeStruct((2, rows, HALF), jnp.float32),
        cost_estimate=pl.CostEstimate(
            flops=2 * 2 * rows * HALF * piece.shape[0], bytes_accessed=2 * rows * piece.shape[0] * 2, transcendentals=0
        ),
        compiler_params=pltpu.CompilerParams(vmem_limit_bytes=8 * MIB),
    )(own, other, piece, *extra)


def near_pairs(stage, by):
    ids = np.arange(np.prod(DIMS)).reshape(DIMS)
    pairs = []
    for core in range(NC):
        along_z = core == stage
        grid = ids[..., core].reshape((NZ, NY) + DIMS[4:6])
        moved = np.roll(grid, -by, axis=0 if along_z else 1)
        pairs += list(zip(grid.ravel().tolist(), moved.ravel().tolist()))
    return sorted(pairs)


def near_shift(x, stage, by):
    return lax.ppermute(x, AXES, near_pairs(stage, by))


def gather_near(x, stage):
    h = x.shape[0] // 2
    first, second, x = lax.optimization_barrier((x[:h], x[h:], x))
    minus, plus = near_shift(x, stage, 1), near_shift(x, stage, -1)
    return minus, plus, near_shift(first, stage, 2), near_shift(second, stage, -2)


def place_of(delta, low):
    w = (delta + low) % NEAR - low
    return jnp.where(w == 0, 0, jnp.where(w == -1, 1, jnp.where(w == 1, 2, 3)))


def positions(masked):
    q = masked
    z, y, xh = q // (NY * NXH), (q // NXH) % NY, q % NXH
    zf, yf = z // NEAR, y // NEAR
    part = zf // 2
    low = 2 - part
    dz = (z - lax.axis_index(Z)) % NZ
    dy = (y - lax.axis_index(Y)) % NY
    core = lax.axis_index("c")
    first = place_of(jnp.where(core == 0, dz, dy), 2)
    second = place_of(jnp.where(core == 0, dy, dz), low)
    pos = second * 64 + part * 32 + first * 8 + (zf % 2) * 4 + yf * NXH + xh
    return jnp.where(q < CLUSTERS, pos, CLUSTERS).astype(jnp.int32)


def per_device(x_panel, b_panel, a_blocks, a_inner, a_count):
    rows, _, slots, bs, _ = a_blocks.shape
    xh = lax.axis_index("xh")
    live = lax.broadcasted_iota(jnp.int32, a_inner.shape, 2) < a_count[:, :, None]
    masked = jnp.where(live, a_inner, CLUSTERS)

    left, right = b_panel[:, :HALF], b_panel[:, HALF:]
    got = lax.ppermute(jnp.where(xh == 0, right, left), "xh", [(0, 1), (1, 0)])
    mine = jnp.where(xh == 0, left, right)
    pair = jnp.where(xh == 0, jnp.concatenate([mine, got]), jnp.concatenate([got, mine]))
    split = rows // 2
    low, high = pack(a_blocks, masked, 0, split), pack(a_blocks, masked, split, rows - split)
    pair, low, high = lax.optimization_barrier((pair, low, high))
    low_other = lax.ppermute(low, "xh", [(0, 1), (1, 0)])
    sent = jnp.broadcast_to(pair[None], (NZF * NYF,) + pair.shape)
    block = lax.all_to_all(sent, ("zf", "yf"), 0, 0, tiled=False).reshape(-1, HALF)
    own = spread(low, high, positions(masked[:, 0, :]))

    block, own = lax.optimization_barrier((block, own))
    h = block.shape[0] // 2
    twice, minus = near_shift(block, 0, 2), near_shift(block, 0, 1)
    block, low_other, high = lax.optimization_barrier((block, low_other, high))
    plus = near_shift(block, 0, -1)
    high_other = lax.ppermute(high, "xh", [(0, 1), (1, 0)])
    plane = jnp.concatenate(
        [block[:h], minus[:h], plus[:h], twice[:h], block[h:], minus[h:], plus[h:], twice[h:]]
    )
    pieces = gather_near(plane, 1)

    masked_other = jnp.concatenate([p[:, slots // 2, 0, :slots] for p in (low_other, high_other)]).astype(jnp.int32)
    other = spread(low_other, high_other, positions(masked_other))
    acc = multiply(own, other, plane, 0, None)
    for piece, at in zip(pieces, (64, 128, 192, 224)):
        acc = multiply(own, other, piece, at, acc)

    ordered = jnp.where(xh == 0, acc, acc[::-1])
    back = lax.all_to_all(ordered.reshape(NXH * rows, bs, HALF), ("xh", "xl", "c"), 0, 0, tiled=False)
    halves = back.reshape(NXH, NXL * NC, bs, HALF).sum(axis=1)
    product = jnp.concatenate([halves[0], halves[1]], axis=-1)
    return (1.5 * x_panel.astype(jnp.float32) - 0.5 * product).astype(jnp.bfloat16)


def solution(mesh):
    fine = Mesh(mesh.devices.reshape(DIMS), AXES)
    grid, layer = Z + Y + ("xh",), ("xl", "c")
    placed = (
        P(grid + layer, None),
        P(grid + layer, None),
        P(grid, layer, None, None, None),
        P(grid, layer, None),
        P(grid, layer),
    )
    return jax.shard_map(
        per_device,
        mesh=fine,
        in_specs=placed,
        out_specs=P(grid + layer, None),
        check_vma=False,
    )
```
